32 devices in a mesh: groups: 2 (over x), tensor: 16 (over z, y, core).
Axes of the slice: x: 2, y: 2, z: 4, core: 2. Of those that a mesh axis runs over, the one named last changes fastest.
Arguments:
- up_inputs: bfloat16 [32, 128, 8192], P('groups', None, 'tensor'), parts along dimension 0, may hold values from -6 to 6
- up_grads: bfloat16 [32, 128, 28672], P('groups', None, 'tensor'), parts along dimension 0, may hold values from -6 to 6
- down_inputs: bfloat16 [32, 128, 28672], P('groups', None, 'tensor'), parts along dimension 0, may hold values from -6 to 6
- down_grads: bfloat16 [32, 128, 8192], P('groups', None, 'tensor'), parts along dimension 0, may hold values from -6 to 6
- token_counts: int32 [32], P(('groups', 'tensor')), parts along dimension 0, may hold values from 32 to 128, as said below
- pad_offsets: int32 [32], P(('groups', 'tensor')), parts along dimension 0, may hold values from 0 to 96
- sketch_in_up: bfloat16 [8192, 64], P('tensor'), may hold values from -0.0625 to 0.0625
- sketch_out_up: bfloat16 [28672, 64], P('tensor'), may hold values from -0.03125 to 0.03125
- sketch_in_down: bfloat16 [28672, 64], P('tensor'), may hold values from -0.03125 to 0.03125
- sketch_out_down: bfloat16 [8192, 64], P('tensor'), may hold values from -0.0625 to 0.0625
- queries: bfloat16 [64, 8192], P('tensor'), may hold values from -0.0078125 to 0.0078125
Outputs:
- scores: float32 [32, 64], P(('groups', 'tensor')), parts along dimension 0
The draws below stay inside these ranges and needn't reach their ends.
There are 2 independent parts, one for each index of `groups`. The reference program is written for one: setup_inputs(seed, part) draws one part's arguments, and reference() takes and returns one part's arrays. A program takes and returns all parts, laid end to end along the dimension named above; an argument that names none is the same for every part. Nothing has to cross between parts.
Inputs may be any that keep to these rules, and one draw needn't show every extreme that they name: token_counts[e] + pad_offsets[e] <= 128; some example has all 128 slots live.
All inputs are finite; a program needn't handle non-finite values.
Results may differ from the reference program's by a relative error of at most 0.0029.
Values may be sent and summed in bfloat16 or wider, within the bound.
A program may use at most 128 MiB of HBM per device.

```python
import jax
import jax.numpy as jnp
from jax import lax

D = 8192
FF = 28672
R = 64
SEQ = 128
EXAMPLES = 16
NQ = 64


def ragged_pair(key):
    counts = jax.random.randint(jax.random.fold_in(key, 5), (EXAMPLES,), SEQ // 4, SEQ + 1)
    index = jnp.arange(EXAMPLES)
    counts = jnp.where(index == 0, SEQ, counts)
    counts = jnp.where(index == 1, SEQ // 4, counts).astype(jnp.int32)
    offsets = jax.random.randint(jax.random.fold_in(key, 9), (EXAMPLES,), 0, SEQ - counts + 1)
    offsets = jnp.where(index == 1, SEQ - SEQ // 4, offsets)
    return (counts, offsets.astype(jnp.int32))


def draw_token_counts(key, part):
    return ragged_pair(key)[0]


def draw_pad_offsets(key, part):
    return ragged_pair(key)[1]


def levels(rng, shape, split, low, largest):
    def one(axis_at, parts):
        draws = jax.random.uniform(jax.random.fold_in(jax.random.fold_in(rng, 6), axis_at), (parts,), jnp.float32, low / len(split), largest / len(split))
        return jnp.repeat(jnp.exp(draws), shape[axis_at] // parts).reshape((-1,) + (1,) * (len(shape) - axis_at - 1))

    level = one(*split[0])
    for cut in split[1:]:
        level = level * one(*cut)
    return level


def scatter_about(own_key, extent, spread, limit, shards=(), kind=jnp.bfloat16):
    loudness = levels(own_key, extent, shards, -0.22, 0.18) if shards else 1.0
    values = jax.random.normal(own_key, extent, jnp.float32) * spread * loudness
    return jnp.minimum(jnp.maximum(values, -limit), limit).astype(kind)


def setup_inputs(seed: int = 0, part: int = 0) -> dict:
    splits = jax.random.split(jax.random.key(seed), 12)
    part_keys = jax.random.split(jax.random.fold_in(splits[11], part), 12)
    up_inputs = scatter_about(part_keys[0], (EXAMPLES, SEQ, D), 1.0, 6.0, ((2, 16),))
    up_grads = scatter_about(part_keys[1], (EXAMPLES, SEQ, FF), 1.0, 6.0, ((2, 16),))
    down_inputs = scatter_about(part_keys[2], (EXAMPLES, SEQ, FF), 1.0, 6.0, ((2, 16),))
    down_grads = scatter_about(part_keys[3], (EXAMPLES, SEQ, D), 1.0, 6.0, ((2, 16),))
    token_counts = draw_token_counts(jax.random.fold_in(jax.random.fold_in(splits[11], part), 71), part)
    pad_offsets = draw_pad_offsets(jax.random.fold_in(jax.random.fold_in(splits[11], part), 71), part)
    sketch_in_up = scatter_about(splits[6], (D, R), D ** -0.5, 0.0625, ((0, 16),))
    sketch_out_up = scatter_about(splits[7], (FF, R), FF ** -0.5, 0.03125, ((0, 16),))
    sketch_in_down = scatter_about(splits[8], (FF, R), FF ** -0.5, 0.03125, ((0, 16),))
    sketch_out_down = scatter_about(splits[9], (D, R), D ** -0.5, 0.0625, ((0, 16),))
    queries = scatter_about(splits[10], (NQ, 2 * R * R), (R * R * SEQ) ** -0.5, 0.0078125, ((0, 16),))
    return {"up_inputs": up_inputs, "up_grads": up_grads, "down_inputs": down_inputs, "down_grads": down_grads, "token_counts": token_counts, "pad_offsets": pad_offsets, "sketch_in_up": sketch_in_up, "sketch_out_up": sketch_out_up, "sketch_in_down": sketch_in_down, "sketch_out_down": sketch_out_down, "queries": queries}


def project(acts, grads, p_in, p_out):
    ex, sl, _ = acts.shape
    outs = jnp.dot(grads.reshape(ex * sl, -1), p_out, preferred_element_type=jnp.float32)
    ins = jnp.dot(acts.reshape(ex * sl, -1), p_in, preferred_element_type=jnp.float32)
    return jnp.concatenate([outs, ins], axis=1).reshape(ex, sl, -1)


def outer_sum(proj, live):
    width = proj.shape[2] // 2
    outs = proj[:, :, :width] * live[:, :, None]
    ins = proj[:, :, width:]
    sk = jnp.einsum("esi,esj->eij", outs, ins, precision=lax.Precision.HIGHEST)
    return sk.reshape(proj.shape[0], width * width)


def reference(up_inputs, up_grads, down_inputs, down_grads, token_counts, pad_offsets, sketch_in_up, sketch_out_up, sketch_in_down, sketch_out_down, queries):
    slots = jnp.arange(SEQ, dtype=jnp.int32)[None, :]
    live = ((slots >= pad_offsets[:, None]) & (slots < pad_offsets[:, None] + token_counts[:, None])).astype(jnp.float32)
    first = project(up_inputs, up_grads, sketch_in_up, sketch_out_up)
    second = project(down_inputs, down_grads, sketch_in_down, sketch_out_down)
    train = jnp.concatenate([outer_sum(first, live), outer_sum(second, live)], axis=1).astype(jnp.bfloat16)
    return lax.dot_general(train, queries, (((1,), (1,)), ((), ())), preferred_element_type=jnp.float32)
```

```python
import functools

import jax
import jax.numpy as jnp
from jax import lax
from jax.experimental import pallas as pl
from jax.experimental.pallas import tpu as pltpu
from jax.sharding import PartitionSpec as P

Y_TYPE = jnp.bfloat16
Z_TYPE = jnp.float32
MESH = pl.DeviceIdType.MESH
F32 = jnp.float32


def kernel(
    nz,
    upi, upg, dni, dng, cnt, off, siu, sou, sid, sod, q, out,
    v_upi, v_upg, v_dni, v_dng, r_siu, r_sou, r_sid, r_sod, w_out, w_in,
    csend, crecv, own, ysend, yrecv, zsend, zrecv, qraw, qf, qall, sk, acc,
    in_sem, w_sem, q_sem, c_ss, c_rs, y_ss, y_rs, z_ss, z_rs, qz_ss, qz_rs, qx_ss, qx_rs,
):
    g = lax.axis_index("groups")
    me = lax.axis_index("tensor")
    c = lax.rem(me, 2)
    y = lax.rem(me // 2, 2)
    z = me // 4
    kd = upi.shape[2]
    kf = upg.shape[2]
    r = siu.shape[1]
    seq = upi.shape[1]
    nqd = q.shape[0]
    tiles = q.shape[1] // 128

    def at(zz, yy, cc):
        return (g, (zz * 2 + yy) * 2 + cc)

    def zline(j):
        return lax.rem(z + 1 + j, nz)

    q_copy = pltpu.make_async_copy(q, qraw, q_sem)
    q_copy.start()
    w_copies = [
        pltpu.make_async_copy(a, b, w_sem.at[i])
        for i, (a, b) in enumerate(((sou, r_sou), (sod, r_sod), (siu, r_siu), (sid, r_sid)))
    ]
    for w in w_copies:
        w.start()
    loads = []
    for s in range(nz):
        for h in range(2):
            for yy in range(2):
                p = s * 4 + h * 2 + yy
                e = (zline(s) * 2 + (y if yy else 1 - y)) * 2 + (c if h else 1 - c)
                group = [
                    pltpu.make_async_copy(a.at[e], b.at[p], in_sem.at[p, i])
                    for i, (a, b) in enumerate(((upg, v_upg), (dng, v_dng), (upi, v_upi), (dni, v_dni)))
                ]
                for x in group:
                    x.start()
                loads.append(group)

    barrier = pltpu.get_barrier_semaphore()
    pl.semaphore_signal(barrier, inc=1, device_id=at(z, y, 1 - c), device_id_type=MESH)
    pl.semaphore_signal(barrier, inc=1, device_id=at(z, 1 - y, c), device_id_type=MESH)
    for j in range(nz - 1):
        pl.semaphore_signal(barrier, inc=1, device_id=at(zline(j), y, c), device_id_type=MESH)

    q_copy.wait()
    for m in range(tiles):
        qf[pl.ds(m, nqd, stride=tiles), :] = qraw[:, m * 128 : (m + 1) * 128].astype(F32)
    qall[c, y, z] = qf[...].astype(jnp.bfloat16)

    pl.semaphore_wait(barrier, nz + 1)

    q_z = []
    for j in range(nz - 1):
        copy = pltpu.make_async_remote_copy(
            src_ref=qall.at[c, y, z], dst_ref=qall.at[c, y, z],
            send_sem=qz_ss.at[j], recv_sem=qz_rs.at[j],
            device_id=at(zline(j), y, c), device_id_type=MESH,
        )
        copy.start()
        q_z.append(copy)

    for w in w_copies:
        w.wait()
    w_out[:kf, :] = jnp.concatenate([r_sou[...], jnp.zeros((kf, r), jnp.bfloat16)], axis=1)
    w_out[kf:, :] = jnp.concatenate([jnp.zeros((kd, r), jnp.bfloat16), r_sod[...]], axis=1)
    w_in[:kd, :] = jnp.concatenate([r_siu[...], jnp.zeros((kd, r), jnp.bfloat16)], axis=1)
    w_in[kd:, :] = jnp.concatenate([jnp.zeros((kf, r), jnp.bfloat16), r_sid[...]], axis=1)

    c_copies, y_copies, z_copies = [], [], []

    def finish(s):
        y_copies[s].wait_recv()
        total = own[s, 1] + yrecv[s].astype(F32)
        if s == nz - 1:
            return total
        zsend[s] = total.astype(Z_TYPE)
        copy = pltpu.make_async_remote_copy(
            src_ref=zsend.at[s], dst_ref=zrecv.at[s],
            send_sem=z_ss.at[s], recv_sem=z_rs.at[s],
            device_id=at(zline(s), y, c), device_id_type=MESH,
        )
        copy.start()
        z_copies.append(copy)
        return None

    q_y = pltpu.make_async_remote_copy(
        src_ref=qall.at[c, y], dst_ref=qall.at[c, y],
        send_sem=qx_ss.at[0], recv_sem=qx_rs.at[0],
        device_id=at(z, 1 - y, c), device_id_type=MESH,
    )
    q_c = pltpu.make_async_remote_copy(
        src_ref=qall.at[c], dst_ref=qall.at[c],
        send_sem=qx_ss.at[1], recv_sem=qx_rs.at[1],
        device_id=at(z, y, 1 - c), device_id_type=MESH,
    )

    for s in range(nz):
        for h in range(2):
            p = s * 4 + h * 2
            for group in loads[p : p + 2]:
                for x in group:
                    x.wait()

            def dot(v, w):
                return jnp.dot(v[p : p + 2].reshape(2 * seq, -1), w, preferred_element_type=F32)

            outs = dot(v_upg, w_out[:kf, :]) + dot(v_dng, w_out[kf:, :])
            ins = dot(v_upi, w_in[:kd, :]) + dot(v_dni, w_in[kd:, :])
            dst = own if h else csend
            for yy in range(2):
                dst[s, yy, :, :128] = outs[yy * seq : (yy + 1) * seq]
                dst[s, yy, :, 128:] = ins[yy * seq : (yy + 1) * seq]
            if h == 0:
                copy = pltpu.make_async_remote_copy(
                    src_ref=csend.at[s], dst_ref=crecv.at[s],
                    send_sem=c_ss.at[s], recv_sem=c_rs.at[s],
                    device_id=at(z, y, 1 - c), device_id_type=MESH,
                )
                copy.start()
                c_copies.append(copy)
        c_copies[s].wait_recv()
        ysend[s] = (own[s, 0] + crecv[s, 0]).astype(Y_TYPE)
        copy = pltpu.make_async_remote_copy(
            src_ref=ysend.at[s], dst_ref=yrecv.at[s],
            send_sem=y_ss.at[s], recv_sem=y_rs.at[s],
            device_id=at(z, 1 - y, c), device_id_type=MESH,
        )
        copy.start()
        y_copies.append(copy)
        own[s, 1] = own[s, 1] + crecv[s, 1]
        if s == 1:
            for copy in q_z:
                copy.wait_recv()
            q_y.start()
        if s == 2:
            q_y.wait_recv()
            q_c.start()
        if s >= 1:
            finish(s - 1)

    total = finish(nz - 1)
    for s in range(nz - 1):
        z_copies[s].wait_recv()
        total = total + zrecv[s].astype(F32)

    slot = lax.broadcasted_iota(jnp.int32, (seq, 128), 0)
    first = off[0]
    live = (slot >= first) & (slot < first + cnt[0])
    outs = jnp.where(live, total[:, :128], 0.0)
    sk[...] = lax.dot_general(
        outs, total[:, 128:], (((0,), (0,)), ((), ())),
        precision=lax.Precision.HIGHEST, preferred_element_type=F32,
    )
    half = tiles // 2
    lane = lax.broadcasted_iota(jnp.int32, (half, 128), 1)
    even = sk[pl.ds(0, tiles, stride=2), :]
    odd = sk[pl.ds(1, tiles, stride=2), :]
    train = jnp.concatenate(
        [
            jnp.where(lane < r, even[:half], pltpu.roll(odd[:half], r, 1)),
            jnp.where(lane < r, pltpu.roll(even[half:], r, 1), odd[half:]),
        ],
        axis=0,
    )

    q_c.wait_recv()
    at_row = 0
    for zz in range(nz):
        for yy in range(2):
            for cc in range(2):
                rows = qall[cc, yy, zz].astype(F32).reshape(nqd, tiles, 128)
                acc[at_row : at_row + nqd, :] = jnp.sum(rows * train[None], axis=1)
                at_row += nqd
    out[...] = lax.dot_general(
        jnp.ones((8, 128), F32), acc[...], (((1,), (1,)), ((), ())),
        precision=lax.Precision.HIGHEST, preferred_element_type=F32,
    )[:1]

    for copy in q_z + c_copies + y_copies + z_copies + [q_y, q_c]:
        copy.wait_send()


def local(nz, upi, upg, dni, dng, cnt, off, siu, sou, sid, sod, q):
    ex, seq, kd = upi.shape
    kf = upg.shape[2]
    r = siu.shape[1]
    nqd, width = q.shape
    n = 4 * nz
    bf = jnp.bfloat16
    any_ = pl.BlockSpec(memory_space=pl.ANY)
    smem = pl.BlockSpec(memory_space=pltpu.SMEM)
    dma = pltpu.SemaphoreType.DMA
    return pl.pallas_call(
        functools.partial(kernel, nz),
        out_shape=jax.ShapeDtypeStruct((1, nqd * n), F32),
        in_specs=[any_] * 4 + [smem] * 2 + [any_] * 5,
        out_specs=pl.BlockSpec(memory_space=pltpu.VMEM),
        scratch_shapes=[
            pltpu.VMEM((ex, seq, kd), bf),
            pltpu.VMEM((ex, seq, kf), bf),
            pltpu.VMEM((ex, seq, kf), bf),
            pltpu.VMEM((ex, seq, kd), bf),
            pltpu.VMEM((kd, r), bf),
            pltpu.VMEM((kf, r), bf),
            pltpu.VMEM((kf, r), bf),
            pltpu.VMEM((kd, r), bf),
            pltpu.VMEM((kf + kd, 2 * r), bf),
            pltpu.VMEM((kf + kd, 2 * r), bf),
            pltpu.VMEM((nz, 2, seq, 4 * r), F32),
            pltpu.VMEM((nz, 2, seq, 4 * r), F32),
            pltpu.VMEM((nz, 2, seq, 4 * r), F32),
            pltpu.VMEM((nz, seq, 4 * r), Y_TYPE),
            pltpu.VMEM((nz, seq, 4 * r), Y_TYPE),
            pltpu.VMEM((nz, seq, 4 * r), Z_TYPE),
            pltpu.VMEM((nz, seq, 4 * r), Z_TYPE),
            pltpu.VMEM((nqd, width), bf),
            pltpu.VMEM((nqd * width // 128, 128), F32),
            pltpu.VMEM((2, 2, nz, nqd * width // 128, 128), bf),
            pltpu.VMEM((2 * r, 2 * r), F32),
            pltpu.VMEM((nqd * n, 128), F32),
            dma((ex, 4)),
            dma((4,)),
            dma(()),
            dma((nz,)),
            dma((nz,)),
            dma((nz,)),
            dma((nz,)),
            dma((nz,)),
            dma((nz,)),
            dma((nz,)),
            dma((nz,)),
            dma((2,)),
            dma((2,)),
        ],
        compiler_params=pltpu.CompilerParams(
            collective_id=0, has_side_effects=True, vmem_limit_bytes=50 * 1024 * 1024
        ),
    )(upi, upg, dni, dng, cnt, off, siu, sou, sid, sod, q)


def solution(mesh):
    return jax.shard_map(
        functools.partial(local, mesh.shape["tensor"] // 4),
        mesh=mesh,
        in_specs=(
            P("groups", None, "tensor"),
            P("groups", None, "tensor"),
            P("groups", None, "tensor"),
            P("groups", None, "tensor"),
            P(("groups", "tensor")),
            P(("groups", "tensor")),
            P("tensor", None),
            P("tensor", None),
            P("tensor", None),
            P("tensor", None),
            P("tensor", None),
        ),
        out_specs=P(("groups", "tensor"), None),
        check_vma=False,
    )
```

```python
import functools

import jax
import jax.numpy as jnp
from jax import lax
from jax.experimental import pallas as pl
from jax.experimental.pallas import tpu as pltpu
from jax.sharding import PartitionSpec as P

Y_TYPE = jnp.bfloat16
Z_TYPE = jnp.float32
AHEAD = 2
MESH = pl.DeviceIdType.MESH
F32 = jnp.float32


def kernel(
    nz,
    upi, upg, dni, dng, cnt, off, siu, sou, sid, sod, q, out,
    v_upi, v_upg, v_dni, v_dng, v_cnt, v_off, w_out, w_in,
    csend, crecv, own, ysend, yrecv, zsend, zrecv, qraw, qf, qall, sk, acc,
    in_sem, w_sem, q_sem, n_sem, c_ss, c_rs, y_ss, y_rs, z_ss, z_rs, qz_ss, qz_rs, qx_ss, qx_rs,
):
    g = lax.axis_index("groups")
    me = lax.axis_index("tensor")
    c = lax.rem(me, 2)
    y = lax.rem(me // 2, 2)
    z = me // 4
    kd = upi.shape[2]
    kf = upg.shape[2]
    r = siu.shape[0]
    seq = upi.shape[1]
    nqd = q.shape[0]
    tiles = q.shape[1] // 128

    def at(zz, yy, cc):
        return (g, (zz * 2 + yy) * 2 + cc)

    shifts = sorted(range(1, nz), key=lambda k: -min(k, nz - k)) + [nz]

    def zline(j):
        return lax.rem(z + shifts[j], nz)

    q_copy = pltpu.make_async_copy(q, qraw, q_sem)
    q_copy.start()
    w_copies = [
        pltpu.make_async_copy(a, b, w_sem.at[i])
        for i, (a, b) in enumerate(
            (
                (sou, w_out.at[:r, :kf]),
                (sod, w_out.at[r:, kf:]),
                (siu, w_in.at[:r, :kd]),
                (sid, w_in.at[r:, kd:]),
            )
        )
    ]
    n_copies = [
        pltpu.make_async_copy(a, b, n_sem.at[i]) for i, (a, b) in enumerate(((cnt, v_cnt), (off, v_off)))
    ]
    for w in w_copies:
        w.start()
    loads = []
    for s in range(nz):
        for h in range(2):
            for yy in range(2):
                p = s * 4 + h * 2 + yy
                e = (zline(s) * 2 + (y if yy else 1 - y)) * 2 + (c if h else 1 - c)
                group = [
                    pltpu.make_async_copy(a.at[e], b.at[p], in_sem.at[p, i])
                    for i, (a, b) in enumerate(((upg, v_upg), (dng, v_dng), (upi, v_upi), (dni, v_dni)))
                ]
                if s < AHEAD:
                    for x in group:
                        x.start()
                loads.append(group)

    barrier = pltpu.get_barrier_semaphore()
    pl.semaphore_signal(barrier, inc=1, device_id=at(z, y, 1 - c), device_id_type=MESH)
    pl.semaphore_signal(barrier, inc=1, device_id=at(z, 1 - y, c), device_id_type=MESH)
    for j in range(nz - 1):
        pl.semaphore_signal(barrier, inc=1, device_id=at(zline(j), y, c), device_id_type=MESH)

    for w in n_copies:
        w.start()
    w_out[r:, :kf] = jnp.zeros((r, kf), jnp.bfloat16)
    w_out[:r, kf:] = jnp.zeros((r, kd), jnp.bfloat16)
    w_in[r:, :kd] = jnp.zeros((r, kd), jnp.bfloat16)
    w_in[:r, kd:] = jnp.zeros((r, kf), jnp.bfloat16)

    q_copy.wait()
    for m in range(tiles):
        qf[pl.ds(m, nqd, stride=tiles), :] = qraw[:, m * 128 : (m + 1) * 128].astype(F32)
    qall[c, y, z] = qf[...].astype(jnp.bfloat16)

    pl.semaphore_wait(barrier, nz + 1)

    q_z = []
    for j in range(nz - 1):
        copy = pltpu.make_async_remote_copy(
            src_ref=qall.at[c, y, z], dst_ref=qall.at[c, y, z],
            send_sem=qz_ss.at[j], recv_sem=qz_rs.at[j],
            device_id=at(zline(j), y, c), device_id_type=MESH,
        )
        copy.start()
        q_z.append(copy)

    for w in w_copies:
        w.wait()

    c_copies, y_copies, z_copies = [], [], []

    def finish(s):
        y_copies[s].wait_recv()
        total = own[s, 1] + yrecv[s].astype(F32)
        if s == nz - 1:
            return total
        zsend[s] = total.astype(Z_TYPE)
        copy = pltpu.make_async_remote_copy(
            src_ref=zsend.at[s], dst_ref=zrecv.at[s],
            send_sem=z_ss.at[s], recv_sem=z_rs.at[s],
            device_id=at(zline(s), y, c), device_id_type=MESH,
        )
        copy.start()
        z_copies.append(copy)
        return None

    q_y = pltpu.make_async_remote_copy(
        src_ref=qall.at[c, y], dst_ref=qall.at[c, y],
        send_sem=qx_ss.at[0], recv_sem=qx_rs.at[0],
        device_id=at(z, 1 - y, c), device_id_type=MESH,
    )
    q_c = pltpu.make_async_remote_copy(
        src_ref=qall.at[c], dst_ref=qall.at[c],
        send_sem=qx_ss.at[1], recv_sem=qx_rs.at[1],
        device_id=at(z, y, 1 - c), device_id_type=MESH,
    )

    for s in range(nz):
        for group in loads[4 * (s + AHEAD) : 4 * (s + AHEAD + 1)]:
            for x in group:
                x.start()
        for h in range(2):
            p = s * 4 + h * 2
            for group in loads[p : p + 2]:
                for x in group:
                    x.wait()

            def dot(v, w):
                return lax.dot_general(
                    v[p : p + 2].reshape(2 * seq, -1), w, (((1,), (1,)), ((), ())), preferred_element_type=F32
                )

            outs = dot(v_upg, w_out[:, :kf]) + dot(v_dng, w_out[:, kf:])
            ins = dot(v_upi, w_in[:, :kd]) + dot(v_dni, w_in[:, kd:])
            dst = own if h else csend
            for yy in range(2):
                dst[s, yy, :, :128] = outs[yy * seq : (yy + 1) * seq]
                dst[s, yy, :, 128:] = ins[yy * seq : (yy + 1) * seq]
            if h == 0:
                copy = pltpu.make_async_remote_copy(
                    src_ref=csend.at[s], dst_ref=crecv.at[s],
                    send_sem=c_ss.at[s], recv_sem=c_rs.at[s],
                    device_id=at(z, y, 1 - c), device_id_type=MESH,
                )
                copy.start()
                c_copies.append(copy)
                if s >= 1:
                    finish(s - 1)
        c_copies[s].wait_recv()
        ysend[s] = (own[s, 0] + crecv[s, 0]).astype(Y_TYPE)
        copy = pltpu.make_async_remote_copy(
            src_ref=ysend.at[s], dst_ref=yrecv.at[s],
            send_sem=y_ss.at[s], recv_sem=y_rs.at[s],
            device_id=at(z, 1 - y, c), device_id_type=MESH,
        )
        copy.start()
        y_copies.append(copy)
        own[s, 1] = own[s, 1] + crecv[s, 1]
        if s == nz - 2:
            for copy in q_z:
                copy.wait_recv()
            q_y.start()
        if s == nz - 1:
            q_y.wait_recv()
            q_c.start()

    total = finish(nz - 1)
    for s in range(nz - 1):
        z_copies[s].wait_recv()
        total = total + zrecv[s].astype(F32)

    slot = lax.broadcasted_iota(jnp.int32, (seq, 128), 0)
    for w in n_copies:
        w.wait()
    first = v_off[0]
    live = (slot >= first) & (slot < first + v_cnt[0])
    outs = jnp.where(live, total[:, :128], 0.0)
    sk[...] = lax.dot_general(
        outs, total[:, 128:], (((0,), (0,)), ((), ())),
        precision=lax.Precision.HIGHEST, preferred_element_type=F32,
    )
    half = tiles // 2
    lane = lax.broadcasted_iota(jnp.int32, (half, 128), 1)
    even = sk[pl.ds(0, tiles, stride=2), :]
    odd = sk[pl.ds(1, tiles, stride=2), :]
    train = jnp.concatenate(
        [
            jnp.where(lane < r, even[:half], pltpu.roll(odd[:half], r, 1)),
            jnp.where(lane < r, pltpu.roll(even[half:], r, 1), odd[half:]),
        ],
        axis=0,
    )

    q_c.wait_recv()
    at_row = 0
    for zz in range(nz):
        for yy in range(2):
            for cc in range(2):
                rows = qall[cc, yy, zz].astype(F32).reshape(nqd, tiles, 128)
                acc[at_row : at_row + nqd, :] = jnp.sum(rows * train[None], axis=1)
                at_row += nqd
    out[...] = lax.dot_general(
        jnp.ones((8, 128), F32), acc[...], (((1,), (1,)), ((), ())),
        precision=lax.Precision.HIGHEST, preferred_element_type=F32,
    )[:1]

    for copy in q_z + c_copies + y_copies + z_copies + [q_y, q_c]:
        copy.wait_send()


def local(nz, upi, upg, dni, dng, cnt, off, siu, sou, sid, sod, q):
    siu, sou, sid, sod = siu.T, sou.T, sid.T, sod.T
    ex, seq, kd = upi.shape
    kf = upg.shape[2]
    r = siu.shape[0]
    nqd, width = q.shape
    n = 4 * nz
    bf = jnp.bfloat16
    hbm = pl.BlockSpec(memory_space=pltpu.HBM)
    dma = pltpu.SemaphoreType.DMA
    return pl.pallas_call(
        functools.partial(kernel, nz),
        out_shape=jax.ShapeDtypeStruct((1, nqd * n), F32),
        in_specs=[hbm] * 11,
        out_specs=pl.BlockSpec(memory_space=pltpu.VMEM),
        scratch_shapes=[
            pltpu.VMEM((ex, seq, kd), bf),
            pltpu.VMEM((ex, seq, kf), bf),
            pltpu.VMEM((ex, seq, kf), bf),
            pltpu.VMEM((ex, seq, kd), bf),
            pltpu.SMEM((1,), jnp.int32),
            pltpu.SMEM((1,), jnp.int32),
            pltpu.VMEM((2 * r, kf + kd), bf),
            pltpu.VMEM((2 * r, kf + kd), bf),
            pltpu.VMEM((nz, 2, seq, 4 * r), F32),
            pltpu.VMEM((nz, 2, seq, 4 * r), F32),
            pltpu.VMEM((nz, 2, seq, 4 * r), F32),
            pltpu.VMEM((nz, seq, 4 * r), Y_TYPE),
            pltpu.VMEM((nz, seq, 4 * r), Y_TYPE),
            pltpu.VMEM((nz, seq, 4 * r), Z_TYPE),
            pltpu.VMEM((nz, seq, 4 * r), Z_TYPE),
            pltpu.VMEM((nqd, width), bf),
            pltpu.VMEM((nqd * width // 128, 128), F32),
            pltpu.VMEM((2, 2, nz, nqd * width // 128, 128), bf),
            pltpu.VMEM((2 * r, 2 * r), F32),
            pltpu.VMEM((nqd * n, 128), F32),
            dma((ex, 4)),
            dma((4,)),
            dma(()),
            dma((2,)),
            dma((nz,)),
            dma((nz,)),
            dma((nz,)),
            dma((nz,)),
            dma((nz,)),
            dma((nz,)),
            dma((nz,)),
            dma((nz,)),
            dma((2,)),
            dma((2,)),
        ],
        compiler_params=pltpu.CompilerParams(
            collective_id=0, has_side_effects=True, vmem_limit_bytes=64 * 1024 * 1024 - 65536
        ),
    )(upi, upg, dni, dng, cnt, off, siu, sou, sid, sod, q)


def solution(mesh):
    return jax.shard_map(
        functools.partial(local, mesh.shape["tensor"] // 4),
        mesh=mesh,
        in_specs=(
            P("groups", None, "tensor"),
            P("groups", None, "tensor"),
            P("groups", None, "tensor"),
            P("groups", None, "tensor"),
            P(("groups", "tensor")),
            P(("groups", "tensor")),
            P("tensor", None),
            P("tensor", None),
            P("tensor", None),
            P("tensor", None),
            P("tensor", None),
        ),
        out_specs=P(("groups", "tensor"), None),
        check_vma=False,
    )
```
